256 devices in a mesh: seq: 16 (over z_lo, y), head: 8 (over z_hi, x), cfg: 2 (over core).
Axes of the slice: x: 4, y: 4, z: 8 (z_hi: 2, z_lo: 4; z = z_hi * 4 + z_lo), core: 2. Of those that a mesh axis runs over, the one named last changes fastest.
Arguments:
- queries: bfloat16 [12288, 5120], P(('cfg', 'seq'), 'head'), parts along dimension 0, may hold values from -16 to 16
- fresh_key: bfloat16 [12288, 5120], P(('cfg', 'seq'), 'head'), parts along dimension 0, may hold values from -16 to 16
- fresh_value: bfloat16 [12288, 5120], P(('cfg', 'seq'), 'head'), parts along dimension 0, may hold values from -6 to 6
- stale_key: bfloat16 [12288, 5120], P(('cfg', 'seq'), 'head'), parts along dimension 0, may hold values from -6 to 6
- stale_value: bfloat16 [12288, 5120], P(('cfg', 'seq'), 'head'), parts along dimension 0, may hold values from -6 to 6
- slot_tiles: int32 [96], P('cfg'), parts along dimension 0, may hold values from 0 to 47, as said below
- refresh: int32 [96], P('cfg'), parts along dimension 0, may hold values from 0 to 1, as said below
- stale_reads: int32 [32, 48], P('cfg'), parts along dimension 0, may hold values from 0 to 1, as said below
- out_weight: bfloat16 [5120, 5120], P('head'), may hold values from -6 to 6
Outputs:
- mixed: bfloat16 [12288, 5120], P(('cfg', 'seq', 'head')), parts along dimension 0
The draws below stay inside these ranges and needn't reach their ends.
There are 2 independent parts, one for each index of `cfg`. The reference program is written for one: setup_inputs(seed, part) draws one part's arguments, and reference() takes and returns one part's arrays. A program takes and returns all parts, laid end to end along the dimension named above; an argument that names none is the same for every part. Nothing has to cross between parts.
Inputs may be any that keep to these rules, and one draw needn't show every extreme that they name: `slot_tiles`: A permutation of the 48 tiles. Cache slot i lies on index i // 3 of seq; the slots of every index of seq hold at least one tile that is not refreshed. `refresh`: tile t belongs to index t // 3 of seq. Every index of seq owns between 1 and 2 refreshed tiles; some index owns exactly 1 and some exactly 2. `stale_reads`: only tiles that are not refreshed are read. A reader reads at most one tile among the slots of any one index of seq; some reader reads one tile from the slots of every index.
All inputs are finite; a program needn't handle non-finite values.
Results may differ from the reference program's by a relative error of at most 0.019.
Values may be sent and summed in bfloat16 or wider, within the bound.
A program may use at most 192 MiB of HBM per device.

```python
import jax
import jax.numpy as jnp
from jax import lax

D = 5120
HEADS = 40
HD = 128
TILE = 128
TILE_DEV = 3
TOK_DEV = 384
TOKENS = 6144
TILES = 48
N_SEQ = 16
N_HEAD = 8


def layout(key):
    parts = jax.random.split(jax.random.fold_in(key, 101), 11)
    count = N_SEQ
    place = jnp.arange(TILE_DEV, dtype=jnp.int32)[None, :]
    device = jnp.arange(count, dtype=jnp.int32)[:, None]
    pick = jax.random.randint(parts[0], (count,), 0, TILE_DEV)
    other = jax.random.randint(parts[1], (count,), 0, TILE_DEV - 1)
    forced = (pick + 1 + other) % TILE_DEV
    coins = jax.random.randint(parts[2], (count, TILE_DEV), 0, 2)
    many = jax.random.randint(parts[3], (), 0, count)
    few = (many + 1 + jax.random.randint(parts[4], (), 0, count - 1)) % count
    filled = jnp.where(device == many, 1, jnp.where(device == few, 0, coins))
    fresh = jnp.where(place == forced[:, None], 1, jnp.where(place == pick[:, None], 0, filled))
    refresh = fresh.reshape(TILES).astype(jnp.int32)
    marked = jnp.arange(count, dtype=jnp.int32) * TILE_DEV + pick
    is_marked = jnp.zeros((TILES,), jnp.int32).at[marked].set(1)
    shuffled = jax.random.permutation(parts[5], TILES).astype(jnp.int32)
    ranking = (1 - is_marked) * TILES + shuffled
    order = jnp.argsort(ranking, stable=True).astype(jnp.int32)
    lists = jnp.concatenate([order[:count][:, None], order[count:].reshape(count, TILE_DEV - 1)], axis=1)
    turned = jax.random.randint(parts[6], (count,), 0, TILE_DEV)
    index = (place - turned[:, None]) % TILE_DEV
    slots = jnp.take_along_axis(lists, index, axis=1)
    holder = jnp.arange(count, dtype=jnp.int32)
    first = jax.random.randint(parts[7], (count, count), 0, TILE_DEV)
    candidate = slots[holder[None, :], first]
    fallback = slots[holder, turned][None, :]
    chosen = jnp.where(refresh[candidate] == 0, candidate, fallback)
    rates = jax.random.randint(parts[8], (count,), 3, 11)
    full = jax.random.randint(parts[9], (), 0, count)
    rates = jnp.where(holder == full, 10, rates)
    taken = (jax.random.randint(parts[10], (count, count), 0, 10) < rates[:, None]).astype(jnp.int32)
    rows = jnp.broadcast_to(holder[:, None], (count, count))
    reads = jnp.zeros((count, TILES), jnp.int32).at[rows, chosen].set(taken)
    return (refresh, slots.reshape(TILES).astype(jnp.int32), reads)


def draw_queries(key, part):
    base = jnp.clip(jax.random.normal(jax.random.fold_in(key, 11), (TOKENS, HEADS * HD), jnp.float32), -4.0, 4.0)
    return base.astype(jnp.bfloat16)


def draw_fresh_key(key, part):
    base = jnp.clip(jax.random.normal(jax.random.fold_in(key, 12), (TOKENS, HEADS * HD), jnp.float32), -4.0, 4.0)
    return base.astype(jnp.bfloat16)


def draw_slot_tiles(key, part):
    return layout(key)[1]


def draw_refresh(key, part):
    return layout(key)[0]


def draw_stale_reads(key, part):
    return layout(key)[2]


def block_scale(stream_key, shape, pieces, least, largest):
    def one(position, blocks):
        draws = jax.random.uniform(jax.random.fold_in(jax.random.fold_in(stream_key, 6), position), (blocks,), jnp.float32, least / len(pieces), largest / len(pieces))
        return jnp.repeat(jnp.exp(draws), shape[position] // blocks).reshape((-1,) + (1,) * (len(shape) - position - 1))

    level = one(*pieces[0])
    for cut in pieces[1:]:
        level = level * one(*cut)
    return level


def normal_values(own_key, dims, deviation, limit, cuts=(), kind=jnp.bfloat16):
    values = deviation * jax.random.normal(own_key, dims, jnp.float32)
    if cuts:
        values = values * block_scale(own_key, dims, cuts, -0.22, 0.18)
    return jnp.clip(values, -limit, limit).astype(kind)


def setup_inputs(seed: int = 0, part: int = 0) -> dict:
    key_of = jax.random.split(jax.random.key(seed), 10)
    part_keys = jax.random.split(jax.random.fold_in(key_of[9], part), 10)
    return {
        "queries": draw_queries(jax.random.fold_in(jax.random.fold_in(key_of[9], part), 71), part),
        "fresh_key": draw_fresh_key(jax.random.fold_in(jax.random.fold_in(key_of[9], part), 71), part),
        "fresh_value": normal_values(part_keys[2], (TOKENS, HEADS * HD), 1.0, 6.0, ((0, 16), (1, 8))),
        "stale_key": normal_values(part_keys[3], (TILES * TILE, HEADS * HD), 1.0, 6.0, ((0, 16), (1, 8))),
        "stale_value": normal_values(part_keys[4], (TILES * TILE, HEADS * HD), 1.0, 6.0, ((0, 16), (1, 8))),
        "slot_tiles": draw_slot_tiles(jax.random.fold_in(jax.random.fold_in(key_of[9], part), 71), part),
        "refresh": draw_refresh(jax.random.fold_in(jax.random.fold_in(key_of[9], part), 71), part),
        "stale_reads": draw_stale_reads(jax.random.fold_in(jax.random.fold_in(key_of[9], part), 71), part),
        "out_weight": normal_values(key_of[8], (HEADS * HD, D), ((TOKENS / (2 * HEADS * HD)) ** 0.5), 6.0, ((0, 8),)),
    }


def reference(queries, fresh_key, fresh_value, stale_key, stale_value, slot_tiles, refresh, stale_reads, out_weight):
    width = HEADS * HD
    scale = HD ** -0.5
    fresh_mask = jnp.repeat(refresh, TILE).astype(jnp.float32)
    slot_hit = (slot_tiles[:, None] == jnp.arange(TILES, dtype=jnp.int32)[None, :]).astype(jnp.int32)
    cache_k = stale_key.astype(jnp.float32).reshape(N_SEQ, TILE_DEV, TILE, width)
    cache_v = stale_value.astype(jnp.float32).reshape(N_SEQ, TILE_DEV, TILE, width)
    keys_f = fresh_key.astype(jnp.float32).reshape(TOKENS, HEADS, HD)
    vals_f = fresh_value.astype(jnp.float32).reshape(TOKENS, HEADS, HD)

    def one_reader(reader):
        row = lax.dynamic_slice_in_dim(stale_reads, reader, 1, 0)[0]
        picked = jnp.sum(slot_hit * row[None, :], axis=1).reshape(N_SEQ, TILE_DEV).astype(jnp.float32)
        keys_s = jnp.einsum("hj,hjrc->hrc", picked, cache_k, precision=lax.Precision.HIGHEST).reshape(N_SEQ * TILE, HEADS, HD)
        vals_s = jnp.einsum("hj,hjrc->hrc", picked, cache_v, precision=lax.Precision.HIGHEST).reshape(N_SEQ * TILE, HEADS, HD)
        stale_mask = jnp.repeat(jnp.sum(picked, axis=1), TILE)
        keys_all = jnp.concatenate([keys_f, keys_s], axis=0)
        vals_all = jnp.concatenate([vals_f, vals_s], axis=0)
        mask = jnp.concatenate([fresh_mask, stale_mask], axis=0)
        query = lax.dynamic_slice_in_dim(queries, reader * TOK_DEV, TOK_DEV, 0).astype(jnp.float32).reshape(TOK_DEV, HEADS, HD)
        score = jnp.einsum("qhd,khd->qhk", query, keys_all, precision=lax.Precision.HIGHEST) * scale
        score = jnp.where(mask[None, None, :] > 0, score, -1e30)
        top = jnp.max(score, axis=2, keepdims=True)
        weight = jnp.exp(score - top) * mask[None, None, :]
        total = jnp.sum(weight, axis=2)
        rounded = lax.optimization_barrier(weight.astype(jnp.bfloat16)).astype(jnp.float32)
        summed = jnp.einsum("qhk,khd->qhd", rounded, vals_all, precision=lax.Precision.HIGHEST)
        return (summed / total[:, :, None]).reshape(TOK_DEV, width).astype(jnp.bfloat16)

    attended = lax.map(one_reader, jnp.arange(N_SEQ, dtype=jnp.int32)).reshape(TOKENS, width)
    group = width // N_HEAD
    mixed = jnp.zeros((TOKENS, D), jnp.float32)
    for index in range(N_HEAD):
        partial_sum = jnp.dot(attended[:, index * group:(index + 1) * group], out_weight[index * group:(index + 1) * group], preferred_element_type=jnp.float32)
        mixed = mixed + lax.optimization_barrier(partial_sum.astype(jnp.bfloat16)).astype(jnp.float32)
    return mixed.astype(jnp.bfloat16)
```

```python
import functools
import math

import jax
import jax.numpy as jnp
from jax import lax
from jax.experimental import pallas as pl
from jax.experimental.pallas import tpu as pltpu
from jax.sharding import PartitionSpec as P

HD = 128
TILE = 128
SIDE = 4
MESH = pl.DeviceIdType.MESH
NEG = -1e30
LOG2_SCALE = HD ** (-0.5) * math.log2(math.e)
BF16 = jnp.bfloat16
F32 = jnp.float32


def seq_place():
    me = lax.axis_index("seq")
    return me // SIDE, lax.rem(me, SIDE)


def row_peer(zi, yi, step):
    other = lax.rem(yi + step, SIDE)
    return other, {"seq": zi * SIDE + other}


def column_peer(zi, yi, step):
    other = lax.rem(zi + step, SIDE)
    return other, {"seq": other * SIDE + yi}


def greet(devices):
    barrier = pltpu.get_barrier_semaphore()
    for device in devices:
        pl.semaphore_signal(barrier, inc=1, device_id=device, device_id_type=MESH)
    pl.semaphore_wait(barrier, len(devices))


def remote(src, dst, send_sem, recv_sem, device):
    return pltpu.make_async_remote_copy(
        src_ref=src,
        dst_ref=dst,
        send_sem=send_sem,
        recv_sem=recv_sem,
        device_id=device,
        device_id_type=MESH,
    )


def spread_kernel(
    refresh,
    q_ref,
    fk_ref,
    fv_ref,
    sk_ref,
    sv_ref,
    qall,
    kv,
    qpack,
    pack,
    send_q,
    recv_q,
    send_z,
    recv_z,
    send_kv,
    recv_kv,
):
    zi, yi = seq_place()
    me = zi * SIDE + yi
    heads = q_ref.shape[1] // HD
    last = heads - 1
    for h in range(heads):
        qpack[h] = q_ref[:, h * HD : (h + 1) * HD]
    rows = [row_peer(zi, yi, step) for step in (2, 1, 3)]
    columns = [column_peer(zi, yi, step) for step in (1, 2, 3)]
    greet([device for _, device in rows + columns])
    copies = []
    first = []
    for slot, (other, device) in enumerate(rows):
        copy = remote(
            qpack.at[other], qall.at[zi, yi], send_q.at[slot], recv_q.at[slot], device
        )
        copy.start()
        first.append(copy)
    qall[zi, yi] = qpack[yi]
    qall[zi, last] = qpack[last]

    r0 = refresh[3 * me]
    r1 = refresh[3 * me + 1]
    r2 = refresh[3 * me + 2]
    one = jnp.where(r0 > 0, 0, jnp.where(r1 > 0, 1, 2))
    two = jnp.where(r2 > 0, 2, 1)

    def fill(h):
        cut = slice(h * HD, (h + 1) * HD)
        for kind, (fresh, stale) in enumerate(((fk_ref, sk_ref), (fv_ref, sv_ref))):
            pack[h, kind, 0:TILE] = fresh[one, :, cut]
            pack[h, kind, TILE : 2 * TILE] = fresh[two, :, cut]
            for tile in range(3):
                pack[h, kind, (2 + tile) * TILE : (3 + tile) * TILE] = stale[tile, :, cut]

    for h in range(heads):
        fill(h)
    for slot, (other, device) in enumerate(rows):
        for part, source in enumerate((other, last)):
            copy = remote(
                pack.at[source],
                kv.at[yi, pl.ds(2 * part, 2)],
                send_kv.at[slot, part],
                recv_kv.at[slot, part],
                device,
            )
            copy.start()
            copies.append(copy)
    kv[yi, 0:2] = pack[yi]
    kv[yi, 2:4] = pack[last]
    for copy in first:
        copy.wait_recv()
    for slot, (other, device) in enumerate(columns):
        copy = remote(qall.at[zi], qall.at[zi], send_z.at[slot], recv_z.at[slot], device)
        copy.start()
        copies.append(copy)
    for copy in first:
        copy.wait_send()
    for copy in copies:
        copy.wait()


def spread(refresh, queries, fresh_key, fresh_value, stale_key, stale_value):
    tokens, width = queries.shape
    heads = width // HD
    tiles = [x.reshape(3, TILE, width) for x in (fresh_key, fresh_value, stale_key, stale_value)]
    vmem = pl.BlockSpec(memory_space=pltpu.VMEM)
    return pl.pallas_call(
        spread_kernel,
        out_shape=(
            jax.ShapeDtypeStruct((SIDE, heads, tokens, HD), BF16),
            jax.ShapeDtypeStruct((SIDE, 4, 5 * TILE, HD), BF16),
        ),
        in_specs=[pl.BlockSpec(memory_space=pltpu.SMEM)] + [vmem] * 5,
        out_specs=(vmem, vmem),
        scratch_shapes=[
            pltpu.VMEM((heads, tokens, HD), BF16),
            pltpu.VMEM((heads, 2, 5 * TILE, HD), BF16),
            pltpu.SemaphoreType.DMA((3,)),
            pltpu.SemaphoreType.DMA((3,)),
            pltpu.SemaphoreType.DMA((3,)),
            pltpu.SemaphoreType.DMA((3,)),
            pltpu.SemaphoreType.DMA((3, 2)),
            pltpu.SemaphoreType.DMA((3, 2)),
        ],
        compiler_params=pltpu.CompilerParams(
            collective_id=0, has_side_effects=True, vmem_limit_bytes=48 * 2**20
        ),
        name="spread",
    )(refresh, queries, *tiles)


def attend_kernel(heads, refresh, slots, reads, q_ref, kv, o_ref, lse_ref, keys, values, bias, stats):
    zi, yi = seq_place()
    item = pl.program_id(0)
    zr = item // heads
    place = lax.rem(item, heads)
    is_last = place == heads - 1
    reader = zr * SIDE + jnp.where(is_last, yi, place)
    bank = jnp.where(is_last, 1, 0)
    fresh_rows = SIDE * 2 * TILE

    @pl.when(item == 0)
    def _():
        for part in range(2):
            for source in range(SIDE):
                cut = slice(source * 2 * TILE, (source + 1) * 2 * TILE)
                keys[part, cut] = kv[source, 2 * part, 0 : 2 * TILE]
                values[part, cut] = kv[source, 2 * part + 1, 0 : 2 * TILE]
        for source in range(SIDE):
            base = 3 * (zi * SIDE + source)
            count = refresh[base] + refresh[base + 1] + refresh[base + 2]
            cut = source * 2 * TILE
            bias[0:1, cut : cut + TILE] = jnp.zeros((1, TILE), F32)
            bias[0:1, cut + TILE : cut + 2 * TILE] = jnp.full(
                (1, TILE), jnp.where(count > 1, 0.0, NEG), F32
            )

    for source in range(SIDE):
        base = 3 * (zi * SIDE + source)
        flags = [reads[reader, slots[base + j]] for j in range(3)]
        pick = jnp.where(flags[1] > 0, 1, jnp.where(flags[2] > 0, 2, 0))
        start = pl.multiple_of((2 + pick) * TILE, TILE)
        cut = slice(fresh_rows + source * TILE, fresh_rows + (source + 1) * TILE)
        keys[bank, cut] = kv[source, 2 * bank, pl.ds(start, TILE)]
        values[bank, cut] = kv[source, 2 * bank + 1, pl.ds(start, TILE)]
        used = flags[0] + flags[1] + flags[2]
        bias[0:1, cut] = jnp.full((1, TILE), jnp.where(used > 0, 0.0, NEG), F32)

    k = keys[bank]
    v = values[bank]
    b = bias[0:1, :]
    tokens = q_ref.shape[2]
    lane = lax.broadcasted_iota(jnp.int32, (TILE, HD), 1)
    for part in range(tokens // TILE):
        cut = slice(part * TILE, (part + 1) * TILE)
        score = lax.dot_general(
            q_ref[0, 0, cut], k, (((1,), (1,)), ((), ())), preferred_element_type=F32
        )
        score = score * LOG2_SCALE + b
        top = jnp.max(score, axis=1, keepdims=True)
        weight = jnp.exp2(score - top)
        total = jnp.sum(weight, axis=1, keepdims=True)
        out = lax.dot_general(
            weight.astype(BF16), v, (((1,), (0,)), ((), ())), preferred_element_type=F32
        )
        o_ref[0, 0, cut] = (out / total).astype(BF16)
        stats[cut] = jnp.where(lane == place, top + jnp.log2(total), stats[cut])

    @pl.when(is_last)
    def _():
        lse_ref[0] = stats[...].T[0:8, :]


def attend(refresh, slots, reads, qall, kv):
    side, heads, tokens, _ = qall.shape
    keys = SIDE * 3 * TILE
    spec = pl.BlockSpec((1, 1, tokens, HD), lambda i, *_: (i // heads, lax.rem(i, heads), 0, 0))
    return pl.pallas_call(
        functools.partial(attend_kernel, heads),
        out_shape=(
            jax.ShapeDtypeStruct((side, heads, tokens, HD), BF16),
            jax.ShapeDtypeStruct((side, 8, tokens), F32),
        ),
        grid_spec=pltpu.PrefetchScalarGridSpec(
            num_scalar_prefetch=3,
            grid=(side * heads,),
            in_specs=[spec, pl.BlockSpec(kv.shape, lambda i, *_: (0, 0, 0, 0))],
            out_specs=(spec, pl.BlockSpec((1, 8, tokens), lambda i, *_: (i // heads, 0, 0))),
            scratch_shapes=[
                pltpu.VMEM((2, keys, HD), BF16),
                pltpu.VMEM((2, keys, HD), BF16),
                pltpu.VMEM((8, keys), F32),
                pltpu.VMEM((tokens, HD), F32),
            ],
        ),
        compiler_params=pltpu.CompilerParams(vmem_limit_bytes=48 * 2**20),
        name="attend",
    )(refresh, slots, reads, qall, kv)


def project_kernel(
    o_ref,
    lse_ref,
    w_hbm,
    out_ref,
    w,
    orecv,
    lrecv,
    comb,
    att5,
    att,
    pbuf,
    rbuf,
    fbuf,
    own,
    zsend,
    zrecv,
    w_sem,
    send_o,
    recv_o,
    send_l,
    recv_l,
    send_a,
    recv_a,
    send_far,
    recv_far,
    send_near,
    recv_near,
    send_relay,
    recv_relay,
    send_hi,
    recv_hi,
):
    zi, yi = seq_place()
    head = lax.axis_index("head")
    zh, xi = head // SIDE, lax.rem(head, SIDE)
    right = lax.rem(xi + 1, SIDE)
    left = lax.rem(xi + SIDE - 1, SIDE)
    opposite = lax.rem(xi + 2, SIDE)
    to_right = {"head": zh * SIDE + right}
    to_left = {"head": zh * SIDE + left}
    to_hi = {"head": (1 - zh) * SIDE + xi}
    rows = [row_peer(zi, yi, step) for step in (2, 1, 3)]
    columns = [column_peer(zi, yi, step) for step in (1, 2, 3)]
    heads, tokens = o_ref.shape[1], o_ref.shape[2]
    blocks = pbuf.shape[0]
    part_rows, part_columns = pbuf.shape[3], pbuf.shape[4]

    w_copy = pltpu.make_async_copy(w_hbm, w, w_sem)
    w_copy.start()
    greet([device for _, device in rows + columns] + [to_right, to_left, to_hi])
    copies = []
    for slot, (other, device) in enumerate(columns):
        for src, dst, send, recv in (
            (lse_ref, lrecv, send_l, recv_l),
            (o_ref, orecv, send_o, recv_o),
        ):
            copy = remote(src.at[other], dst.at[zi], send.at[slot], recv.at[slot], device)
            copy.start()
            copies.append(copy)
    orecv[zi] = o_ref[zi]
    lrecv[zi] = lse_ref[zi]
    for copy in copies:
        copy.wait()

    logs = [lrecv[z] for z in range(SIDE)]
    top = functools.reduce(jnp.maximum, logs)
    shares = [jnp.exp2(x - top) for x in logs]
    total = functools.reduce(jnp.add, shares)
    shares = [x / total for x in shares]
    pad = jnp.zeros((HD - 8 * SIDE, tokens), F32)
    factors = jnp.concatenate(shares + [pad], axis=0).T
    for k in range(heads):
        mixed = jnp.zeros((tokens, HD), F32)
        for z in range(SIDE):
            mixed += orecv[z, k].astype(F32) * factors[:, z * 8 + k : z * 8 + k + 1]
        comb[k] = mixed.astype(BF16)
    copies = []
    for slot, (other, device) in enumerate(rows):
        copy = remote(comb.at[other], att5.at[yi], send_a.at[slot], recv_a.at[slot], device)
        copy.start()
        copies.append(copy)
    att5[yi] = comb[yi]
    att5[heads - 1] = comb[heads - 1]
    for copy in copies:
        copy.wait()
    for h in range(heads):
        att[:, h * HD : (h + 1) * HD] = att5[h]
    w_copy.wait()

    def plan(block):
        forward = block < blocks // 2
        ahead, behind = (right, left) if forward else (left, right)
        to_ahead, to_behind = (to_right, to_left) if forward else (to_left, to_right)
        side = 0 if forward else 1
        far = remote(
            pbuf.at[block, opposite], rbuf.at[block], send_far.at[block], recv_far.at[block], to_ahead
        )
        near = remote(
            pbuf.at[block, behind],
            fbuf.at[1 - side, block],
            send_near.at[block],
            recv_near.at[block],
            to_behind,
        )
        relay = remote(
            pbuf.at[block, ahead],
            fbuf.at[side, block],
            send_relay.at[block],
            recv_relay.at[block],
            to_ahead,
        )
        hi = remote(zsend.at[block], zrecv.at[block], send_hi.at[block], recv_hi.at[block], to_hi)
        return ahead, far, near, relay, hi

    plans = [plan(block) for block in range(blocks)]
    order = [0, blocks // 2, 1, blocks // 2 + 1]
    for block in order:
        product = jnp.dot(
            att[...],
            w[:, block * part_columns : (block + 1) * part_columns],
            preferred_element_type=F32,
        ).astype(BF16)
        for g in range(2 * SIDE):
            pbuf[block, g % SIDE, g // SIDE] = product[g * part_rows : (g + 1) * part_rows]
        _, far, near, _, _ = plans[block]
        far.start()
        near.start()
    for block in order:
        ahead, far, _, relay, _ = plans[block]
        far.wait_recv()
        pbuf[block, ahead] = (
            pbuf[block, ahead].astype(F32) + rbuf[block].astype(F32)
        ).astype(BF16)
        relay.start()
    for block in order:
        _, _, near, relay, hi = plans[block]
        near.wait_recv()
        relay.wait_recv()
        for side in range(2):
            own[block, side] = (
                pbuf[block, xi, side].astype(F32)
                + fbuf[0, block, side].astype(F32)
                + fbuf[1, block, side].astype(F32)
            )
        zsend[block] = own[block, 1 - zh].astype(BF16)
        hi.start()
    for block in order:
        hi = plans[block][4]
        hi.wait_recv()
        out_ref[:, block * part_columns : (block + 1) * part_columns] = (
            own[block, zh] + zrecv[block].astype(F32)
        ).astype(BF16)
    for block in order:
        _, far, near, relay, hi = plans[block]
        far.wait_send()
        near.wait_send()
        relay.wait_send()
        hi.wait_send()


def project(o, lse, out_weight):
    side, heads, tokens, _ = o.shape
    depth, width = out_weight.shape
    blocks = 4
    cols = width // blocks
    rows = tokens // (2 * SIDE)
    vmem = pl.BlockSpec(memory_space=pltpu.VMEM)
    dma = pltpu.SemaphoreType.DMA
    return pl.pallas_call(
        project_kernel,
        out_shape=jax.ShapeDtypeStruct((rows, width), BF16),
        in_specs=[vmem, vmem, pl.BlockSpec(memory_space=pl.ANY)],
        out_specs=vmem,
        scratch_shapes=[
            pltpu.VMEM((depth, width), BF16),
            pltpu.VMEM((side, heads, tokens, HD), BF16),
            pltpu.VMEM((side, 8, tokens), F32),
            pltpu.VMEM((heads, tokens, HD), BF16),
            pltpu.VMEM((heads, tokens, HD), BF16),
            pltpu.VMEM((tokens, depth), BF16),
            pltpu.VMEM((blocks, SIDE, 2, rows, cols), BF16),
            pltpu.VMEM((blocks, 2, rows, cols), BF16),
            pltpu.VMEM((2, blocks, 2, rows, cols), BF16),
            pltpu.VMEM((blocks, 2, rows, cols), F32),
            pltpu.VMEM((blocks, rows, cols), BF16),
            pltpu.VMEM((blocks, rows, cols), BF16),
            dma,
        ]
        + [dma((3,))] * 6
        + [dma((blocks,))] * 8,
        compiler_params=pltpu.CompilerParams(
            collective_id=1, has_side_effects=True, vmem_limit_bytes=48 * 2**20
        ),
        name="project",
    )(o, lse, out_weight)


def on_device(
    queries,
    fresh_key,
    fresh_value,
    stale_key,
    stale_value,
    slot_tiles,
    refresh,
    stale_reads,
    out_weight,
):
    qall, kv = spread(refresh, queries, fresh_key, fresh_value, stale_key, stale_value)
    o, lse = attend(refresh, slot_tiles, stale_reads, qall, kv)
    return project(o, lse, out_weight)


def solution(mesh):
    return jax.shard_map(
        on_device,
        mesh=mesh,
        in_specs=(
            P(("cfg", "seq"), "head"),
            P(("cfg", "seq"), "head"),
            P(("cfg", "seq"), "head"),
            P(("cfg", "seq"), "head"),
            P(("cfg", "seq"), "head"),
            P("cfg"),
            P("cfg"),
            P("cfg", None),
            P("head", None),
        ),
        out_specs=P(("cfg", "seq", "head"), None),
        check_vma=False,
    )
```

```python
import functools
import math

import jax
import jax.numpy as jnp
from jax import lax
from jax.experimental import pallas as pl
from jax.experimental.pallas import tpu as pltpu
from jax.sharding import PartitionSpec as P

HD = 128
TILE = 128
SIDE = 4
HEADS = 5
SLOTS = 5
HALVES = 2
BLOCKS = 4
LANES = 256
MESH = pl.DeviceIdType.MESH
NEG = -1e30
LOG2_SCALE = HD ** (-0.5) * math.log2(math.e)
BF16 = jnp.bfloat16
F32 = jnp.float32


def kernel(
    refresh,
    wanted,
    q_hbm,
    fk_hbm,
    fv_hbm,
    sk_hbm,
    sv_hbm,
    w_hbm,
    out_ref,
    qpack,
    fresh,
    pack,
    qall,
    kv,
    keys,
    values,
    bias,
    stats,
    o_own,
    l_own,
    o_near,
    l_near,
    o_far,
    l_far,
    o_merge,
    l_merge,
    comb,
    att5,
    w,
    pbuf,
    rbuf,
    fbuf,
    zsend,
    zrecv,
    local_sem,
    send_sem,
    recv_sem,
):
    me = lax.axis_index("seq")
    head = lax.axis_index("head")
    zi, yi = me // SIDE, lax.rem(me, SIDE)
    zh, xi = head // SIDE, lax.rem(head, SIDE)
    right = lax.rem(xi + 1, SIDE)
    left = lax.rem(xi + SIDE - 1, SIDE)
    opposite = lax.rem(xi + 2, SIDE)
    to_right = {"head": zh * SIDE + right}
    to_left = {"head": zh * SIDE + left}
    to_hi = {"head": (1 - zh) * SIDE + xi}
    z1 = zi + 1 - 2 * lax.rem(zi, 2)
    z2 = lax.rem(zi + 2, SIDE)
    z3 = SIDE - 1 - zi
    to_z1 = {"seq": z1 * SIDE + yi}
    to_z2 = {"seq": z2 * SIDE + yi}
    row = []
    for step in (2, 1, 3):
        other = lax.rem(yi + step, SIDE)
        row.append((other, {"seq": zi * SIDE + other}))
    last = HEADS - 1
    tokens = qpack.shape[1]
    half = tokens // HALVES
    started = []
    count = [0]

    def remote(src, dst, device):
        index = count[0]
        count[0] += 1
        copy = pltpu.make_async_remote_copy(
            src_ref=src,
            dst_ref=dst,
            send_sem=send_sem.at[index],
            recv_sem=recv_sem.at[index],
            device_id=device,
            device_id_type=MESH,
        )
        started.append(copy)
        return copy

    def send(src, dst, device):
        copy = remote(src, dst, device)
        copy.start()
        return copy

    local_count = [0]

    def load(src, dst):
        copy = pltpu.make_async_copy(src, dst, local_sem.at[local_count[0]])
        local_count[0] += 1
        copy.start()
        return copy

    def lanes(h):
        return pl.ds(h * HD, HD)

    q_loads = [load(q_hbm.at[:, lanes(h)], qpack.at[h]) for h in range(HEADS)]
    fresh_loads = [load(x, fresh.at[i]) for i, x in enumerate((fk_hbm, fv_hbm))]
    stale_loads = []
    for h in range(HEADS):
        for kind, x in enumerate((sk_hbm, sv_hbm)):
            stale_loads.append(
                load(x.at[:, lanes(h)], pack.at[h, kind, pl.ds(2 * TILE, 3 * TILE)])
            )

    barrier = pltpu.get_barrier_semaphore()
    peers = [device for _, device in row] + [to_z1, to_z2, to_right, to_left, to_hi]
    for device in peers:
        pl.semaphore_signal(barrier, inc=1, device_id=device, device_id_type=MESH)
    pl.semaphore_wait(barrier, len(peers))

    for copy in q_loads:
        copy.wait()
    row_q = [send(qpack.at[other], qall.at[zi, yi], device) for other, device in row]
    qall[zi, yi] = qpack[yi]
    qall[zi, last] = qpack[last]

    r0 = refresh[3 * me]
    r1 = refresh[3 * me + 1]
    r2 = refresh[3 * me + 2]
    for copy in fresh_loads:
        copy.wait()
    for h in range(HEADS):
        for kind in range(2):
            tile0, tile1, tile2 = [fresh[kind, i, :, h * HD : (h + 1) * HD] for i in range(3)]
            pack[h, kind, 0:TILE] = jnp.where(r0 > 0, tile0, jnp.where(r1 > 0, tile1, tile2))
            pack[h, kind, TILE : 2 * TILE] = jnp.where(r2 > 0, tile2, tile1)
    for copy in stale_loads:
        copy.wait()
    row_kv = []
    for other, device in row:
        for part, source in enumerate((other, last)):
            row_kv.append(send(pack.at[source], kv.at[yi, pl.ds(2 * part, 2)], device))
    w_load = load(w_hbm, w)
    kv[yi, 0:2] = pack[yi]
    kv[yi, 2:4] = pack[last]
    values[:, :, HD:] = jnp.ones((2, values.shape[1], HD), BF16)
    stats[...] = jnp.zeros(stats.shape, F32)

    for copy in row_q:
        copy.wait_recv()
    q_far = send(qall.at[zi], qall.at[zi], to_z2)
    q_near = send(qall.at[zi], qall.at[zi], to_z1)
    q_far.wait_recv()
    q_relay = send(qall.at[z2], qall.at[z2], to_z1)

    for copy in row_kv:
        copy.wait_recv()
    for part in range(2):
        for source in range(SIDE):
            cut = slice(source * 2 * TILE, (source + 1) * 2 * TILE)
            keys[part, cut] = kv[source, 2 * part, 0 : 2 * TILE]
            values[part, cut, 0:HD] = kv[source, 2 * part + 1, 0 : 2 * TILE]
    for source in range(SIDE):
        base = 3 * (zi * SIDE + source)
        filled = refresh[base] + refresh[base + 1] + refresh[base + 2]
        cut = source * 2 * TILE
        bias[0:1, cut : cut + TILE] = jnp.zeros((1, TILE), F32)
        bias[0:1, cut + TILE : cut + 2 * TILE] = jnp.full(
            (1, TILE), jnp.where(filled > 1, 0.0, NEG), F32
        )

    fresh_rows = SIDE * 2 * TILE

    def attend(t, zr, place):
        start_row = pl.multiple_of(jnp.where(t == 0, 1 - zh, zh) * half, half)

        def item(k, carry):
            is_last = jnp.where(k == last, 1, 0)
            reader = zr * SIDE + k * (1 - is_last) + yi * is_last
            for source in range(SIDE):
                base = 3 * (zi * SIDE + source)
                flags = [wanted[reader, base + j] for j in range(3)]
                cut = slice(fresh_rows + source * TILE, fresh_rows + (source + 1) * TILE)

                def pick(kind):
                    tile0, tile1, tile2 = [
                        kv[source, kind, (2 + j) * TILE : (3 + j) * TILE] for j in range(3)
                    ]
                    return jnp.where(flags[1] > 0, tile1, jnp.where(flags[2] > 0, tile2, tile0))

                keys[is_last, cut] = pick(2 * is_last)
                values[is_last, cut, 0:HD] = pick(2 * is_last + 1)
                used = flags[0] + flags[1] + flags[2]
                bias[0:1, cut] = jnp.full((1, TILE), jnp.where(used > 0, 0.0, NEG), F32)
            score = lax.dot_general(
                qall[zr, k, pl.ds(start_row, half)],
                keys[is_last],
                (((1,), (1,)), ((), ())),
                preferred_element_type=F32,
            )
            score = score * LOG2_SCALE + bias[0:1, :]
            top = jnp.max(score, axis=1, keepdims=True)
            weight = jnp.exp2(score - top).astype(BF16)
            both = jnp.dot(weight, values[is_last], preferred_element_type=F32)
            total = both[:, HD:]
            o_own[t, place, k] = (both[:, :HD] / total).astype(BF16)
            lane = lax.broadcasted_iota(jnp.int32, (half, HD), 1)
            stats[0:half] = jnp.where(lane == k, top + jnp.log2(total), stats[0:half])
            return carry

        lax.fori_loop(0, HEADS, item, 0)
        l_own[t, place] = stats[...].T[0:8, :]

    def shares(logs):
        top = functools.reduce(jnp.maximum, logs)
        parts = [jnp.exp2(x - top) for x in logs]
        total = functools.reduce(jnp.add, parts)
        parts = [x / total for x in parts]
        pad = jnp.zeros((HD - 8 * len(logs), LANES), F32)
        return top + jnp.log2(total), jnp.concatenate(parts + [pad], axis=0).T

    def mix(pieces, factors, k):
        mixed = jnp.zeros((half, HD), F32)
        for i, piece in enumerate(pieces):
            mixed += piece.astype(F32) * factors[0:half, 8 * i + k : 8 * i + k + 1]
        return mixed.astype(BF16)

    near_copies = [[], []]
    far_copies = [[], []]
    row_copies = [[], []]

    def return_near(t, place, slot):
        near_copies[t].append(send(o_own.at[t, place], o_near.at[t, slot], to_z1))
        near_copies[t].append(send(l_own.at[t, place], l_near.at[t, slot], to_z1))

    def merge(t):
        for copy in near_copies[t]:
            copy.wait_recv()
        l_merge[t], factors = shares([l_own[t, 2], l_near[t, 1]])
        for k in range(HEADS):
            o_merge[t, k] = mix([o_own[t, 2, k], o_near[t, 1, k]], factors, k)
        far_copies[t].append(send(o_merge.at[t], o_far.at[t], to_z2))
        far_copies[t].append(send(l_merge.at[t], l_far.at[t], to_z2))

    def combine(t):
        for copy in far_copies[t]:
            copy.wait_recv()
        _, factors = shares([l_own[t, 0], l_near[t, 0], l_far[t]])
        for k in range(HEADS):
            comb[t, k] = mix([o_own[t, 0, k], o_near[t, 0, k], o_far[t, k]], factors, k)
        for other, device in row:
            row_copies[t].append(send(comb.at[t, other], att5.at[t, yi], device))
        att5[t, yi] = comb[t, yi]
        att5[t, last] = comb[t, last]

    part_rows, part_columns = pbuf.shape[3], pbuf.shape[4]
    order = (0, BLOCKS // 2, 1, BLOCKS // 2 + 1)
    plans = {}
    for t in range(HALVES):
        for block in order:
            forward = block < BLOCKS // 2
            ahead, behind = (right, left) if forward else (left, right)
            to_ahead, to_behind = (to_right, to_left) if forward else (to_left, to_right)
            side = 0 if forward else 1
            plans[t, block] = (
                ahead,
                remote(pbuf.at[t, block, opposite], rbuf.at[t, block], to_ahead),
                remote(pbuf.at[t, block, behind], fbuf.at[1 - side, t, block], to_behind),
                remote(pbuf.at[t, block, ahead], fbuf.at[side, t, block], to_ahead),
            )
    hi_plans = {block: remote(zsend.at[block], zrecv.at[block], to_hi) for block in order}

    def project(t):
        for copy in row_copies[t]:
            copy.wait_recv()
        att = jnp.concatenate([att5[t, h] for h in range(HEADS)], axis=1)
        for block in order:
            product = jnp.dot(
                att,
                w[:, block * part_columns : (block + 1) * part_columns],
                preferred_element_type=F32,
            ).astype(BF16)
            for x in range(SIDE):
                pbuf[t, block, x] = product[x * part_rows : (x + 1) * part_rows]
            _, far, near, _ = plans[t, block]
            far.start()
            near.start()

    def relay(t):
        for block in order:
            ahead, far, _, onward = plans[t, block]
            far.wait_recv()
            pbuf[t, block, ahead] = (
                pbuf[t, block, ahead].astype(F32) + rbuf[t, block].astype(F32)
            ).astype(BF16)
            onward.start()

    def reduced(t, block):
        _, _, near, onward = plans[t, block]
        near.wait_recv()
        onward.wait_recv()
        return (
            pbuf[t, block, xi].astype(F32)
            + fbuf[0, t, block].astype(F32)
            + fbuf[1, t, block].astype(F32)
        )

    attend(0, zi, 0)
    q_near.wait_recv()
    attend(0, z1, 1)
    return_near(0, 1, 0)
    q_relay.wait_recv()
    attend(0, z3, 3)
    return_near(0, 3, 1)
    attend(0, z2, 2)
    attend(1, z1, 1)
    return_near(1, 1, 0)
    merge(0)
    attend(1, z3, 3)
    return_near(1, 3, 1)
    attend(1, z2, 2)
    combine(0)
    attend(1, zi, 0)
    merge(1)
    w_load.wait()
    project(0)
    relay(0)
    combine(1)
    for block in order:
        zsend[block] = reduced(0, block).astype(BF16)
        hi_plans[block].start()
    project(1)
    relay(1)
    for block in order:
        total = reduced(1, block)
        hi_plans[block].wait_recv()
        out_ref[:, block * part_columns : (block + 1) * part_columns] = (
            total + zrecv[block].astype(F32)
        ).astype(BF16)
    for copy in started:
        copy.wait_send()


def on_device(
    queries,
    fresh_key,
    fresh_value,
    stale_key,
    stale_value,
    slot_tiles,
    refresh,
    stale_reads,
    out_weight,
):
    tokens, width = queries.shape
    depth, columns = out_weight.shape
    half = tokens // HALVES
    rows = half // SIDE
    cols = columns // BLOCKS
    keys = SIDE * 3 * TILE
    tiles = jnp.arange(refresh.shape[0], dtype=jnp.int32)
    held = (slot_tiles[:, None] == tiles[None, :]).astype(jnp.int32)
    wanted = jnp.sum(stale_reads[:, None, :] * held[None, :, :], axis=2)
    dma = pltpu.SemaphoreType.DMA
    vmem = pltpu.VMEM
    smem_spec = pl.BlockSpec(memory_space=pltpu.SMEM)
    any_spec = pl.BlockSpec(memory_space=pl.ANY)
    copies = 3 + 6 + 3 + HALVES * (4 + 2 + 3 + 3 * BLOCKS) + BLOCKS
    return pl.pallas_call(
        kernel,
        out_shape=jax.ShapeDtypeStruct((rows, columns), BF16),
        in_specs=[smem_spec] * 2 + [any_spec] * 6,
        out_specs=pl.BlockSpec(memory_space=pltpu.VMEM),
        scratch_shapes=[
            vmem((HEADS, tokens, HD), BF16),
            vmem((2, 3, TILE, width), BF16),
            vmem((HEADS, 2, SLOTS * TILE, HD), BF16),
            vmem((SIDE, HEADS, tokens, HD), BF16),
            vmem((SIDE, 4, SLOTS * TILE, HD), BF16),
            vmem((2, keys, HD), BF16),
            vmem((2, keys, 2 * HD), BF16),
            vmem((8, keys), F32),
            vmem((LANES, HD), F32),
            vmem((HALVES, SIDE, HEADS, half, HD), BF16),
            vmem((HALVES, SIDE, 8, LANES), F32),
            vmem((HALVES, 2, HEADS, half, HD), BF16),
            vmem((HALVES, 2, 8, LANES), F32),
            vmem((HALVES, HEADS, half, HD), BF16),
            vmem((HALVES, 8, LANES), F32),
            vmem((HALVES, HEADS, half, HD), BF16),
            vmem((HALVES, 8, LANES), F32),
            vmem((HALVES, HEADS, half, HD), BF16),
            vmem((HALVES, HEADS, half, HD), BF16),
            vmem((depth, columns), BF16),
            vmem((HALVES, BLOCKS, SIDE, rows, cols), BF16),
            vmem((HALVES, BLOCKS, rows, cols), BF16),
            vmem((2, HALVES, BLOCKS, rows, cols), BF16),
            vmem((BLOCKS, rows, cols), BF16),
            vmem((BLOCKS, rows, cols), BF16),
            dma((HEADS * 3 + 3,)),
            dma((copies,)),
            dma((copies,)),
        ],
        compiler_params=pltpu.CompilerParams(
            collective_id=0, has_side_effects=True, vmem_limit_bytes=56 * 2**20
        ),
        name="attend_and_project",
    )(
        refresh,
        wanted,
        queries,
        fresh_key.reshape(3, TILE, width),
        fresh_value.reshape(3, TILE, width),
        stale_key,
        stale_value,
        out_weight,
    )


def solution(mesh):
    return jax.shard_map(
        on_device,
        mesh=mesh,
        in_specs=(
            P(("cfg", "seq"), "head"),
            P(("cfg", "seq"), "head"),
            P(("cfg", "seq"), "head"),
            P(("cfg", "seq"), "head"),
            P(("cfg", "seq"), "head"),
            P("cfg"),
            P("cfg"),
            P("cfg", None),
            P("head", None),
        ),
        out_specs=P(("cfg", "seq", "head"), None),
        check_vma=False,
    )
```

```python
import functools
import math

import jax
import jax.numpy as jnp
from jax import lax
from jax.experimental import pallas as pl
from jax.experimental.pallas import tpu as pltpu
from jax.sharding import PartitionSpec as P

HD = 128
TILE = 128
SIDE = 4
HEADS = 5
SLOTS = 5
HALVES = 2
BLOCKS = 4
GROUP = 4
LANES = 256
MESH = pl.DeviceIdType.MESH
NEG = -1e30
LOG2_SCALE = HD ** (-0.5) * math.log2(math.e)
BF16 = jnp.bfloat16
F32 = jnp.float32


def kernel(
    refresh,
    wanted,
    q_hbm,
    fk_hbm,
    fv_hbm,
    sk_hbm,
    sv_hbm,
    w_hbm,
    out_ref,
    qpack,
    fresh,
    pack,
    qall,
    kv,
    keys,
    values,
    bias,
    stats,
    o_own,
    l_own,
    o_near,
    l_near,
    o_far,
    l_far,
    o_merge,
    l_merge,
    comb,
    att5,
    w,
    pbuf,
    rbuf,
    fbuf,
    zsend,
    zrecv,
    local_sem,
    send_sem,
    recv_sem,
):
    me = lax.axis_index("seq")
    head = lax.axis_index("head")
    zi, yi = me // SIDE, lax.rem(me, SIDE)
    zh, xi = head // SIDE, lax.rem(head, SIDE)
    right = lax.rem(xi + 1, SIDE)
    left = lax.rem(xi + SIDE - 1, SIDE)
    opposite = lax.rem(xi + 2, SIDE)
    to_right = {"head": zh * SIDE + right}
    to_left = {"head": zh * SIDE + left}
    to_hi = {"head": (1 - zh) * SIDE + xi}
    z1 = zi + 1 - 2 * lax.rem(zi, 2)
    z2 = lax.rem(zi + 2, SIDE)
    z3 = SIDE - 1 - zi
    to_z1 = {"seq": z1 * SIDE + yi}
    to_z2 = {"seq": z2 * SIDE + yi}
    row = []
    for step in (2, 1, 3):
        other = lax.rem(yi + step, SIDE)
        row.append((other, {"seq": zi * SIDE + other}))
    last = HEADS - 1
    tokens = qpack.shape[1]
    half = tokens // HALVES
    started = []
    count = [0]

    def remote(src, dst, device):
        index = count[0]
        count[0] += 1
        copy = pltpu.make_async_remote_copy(
            src_ref=src,
            dst_ref=dst,
            send_sem=send_sem.at[index],
            recv_sem=recv_sem.at[index],
            device_id=device,
            device_id_type=MESH,
        )
        started.append(copy)
        return copy

    def send(src, dst, device):
        copy = remote(src, dst, device)
        copy.start()
        return copy

    local_count = [0]

    def load(src, dst):
        copy = pltpu.make_async_copy(src, dst, local_sem.at[local_count[0]])
        local_count[0] += 1
        copy.start()
        return copy

    def lanes(h):
        return pl.ds(h * HD, HD)

    q_loads = [load(q_hbm.at[:, lanes(h)], qpack.at[h]) for h in range(HEADS)]
    fresh_loads = [load(x, fresh.at[i]) for i, x in enumerate((fk_hbm, fv_hbm))]
    stale_loads = []
    for h in range(HEADS):
        for kind, x in enumerate((sk_hbm, sv_hbm)):
            stale_loads.append(
                load(x.at[:, lanes(h)], pack.at[h, kind, pl.ds(2 * TILE, 3 * TILE)])
            )

    barrier = pltpu.get_barrier_semaphore()
    peers = [device for _, device in row] + [to_z1, to_z2, to_right, to_left, to_hi]
    for device in peers:
        pl.semaphore_signal(barrier, inc=1, device_id=device, device_id_type=MESH)
    pl.semaphore_wait(barrier, len(peers))

    for copy in q_loads:
        copy.wait()
    row_q = [send(qpack.at[other], qall.at[zi, yi], device) for other, device in row]
    qall[zi, yi] = qpack[yi]
    qall[zi, last] = qpack[last]

    r0 = refresh[3 * me]
    r1 = refresh[3 * me + 1]
    r2 = refresh[3 * me + 2]
    for copy in fresh_loads:
        copy.wait()
    for h in range(HEADS):
        for kind in range(2):
            tile0, tile1, tile2 = [fresh[kind, i, :, h * HD : (h + 1) * HD] for i in range(3)]
            pack[h, kind, 0:TILE] = jnp.where(r0 > 0, tile0, jnp.where(r1 > 0, tile1, tile2))
            pack[h, kind, TILE : 2 * TILE] = jnp.where(r2 > 0, tile2, tile1)
    for copy in stale_loads:
        copy.wait()
    row_kv = [
        [send(pack.at[other], kv.at[yi, pl.ds(0, 2)], device) for other, device in row],
        [send(pack.at[last], kv.at[yi, pl.ds(2, 2)], device) for _, device in row],
    ]
    w_load = load(w_hbm, w)
    kv[yi, 0:2] = pack[yi]
    kv[yi, 2:4] = pack[last]
    values[:, :, :, HD:] = jnp.ones((2, GROUP, values.shape[2], HD), BF16)
    stats[...] = jnp.zeros(stats.shape, F32)

    for copy in row_q:
        copy.wait_recv()
    starts = [pl.multiple_of((1 - zh) * half, half), pl.multiple_of(zh * half, half)]

    def give_q(t, zr, device):
        part = qall.at[zr, :, pl.ds(starts[t], half)]
        return send(part, part, device)

    q_far = [give_q(0, zi, to_z2), None]
    q_near = [give_q(0, zi, to_z1), None]
    q_far[0].wait_recv()
    q_relay = [give_q(0, z2, to_z1), None]
    q_far[1] = give_q(1, zi, to_z2)
    q_near[1] = give_q(1, zi, to_z1)

    def gather_fresh(part):
        for copy in row_kv[part]:
            copy.wait_recv()
        for source in range(SIDE):
            cut = slice(source * 2 * TILE, (source + 1) * 2 * TILE)
            fresh_keys = kv[source, 2 * part, 0 : 2 * TILE]
            fresh_values = kv[source, 2 * part + 1, 0 : 2 * TILE]
            for g in range(GROUP):
                keys[part, g, cut] = fresh_keys
                values[part, g, cut, 0:HD] = fresh_values

    for source in range(SIDE):
        base = 3 * (zi * SIDE + source)
        filled = refresh[base] + refresh[base + 1] + refresh[base + 2]
        cut = source * 2 * TILE
        for g in range(GROUP):
            bias[g, 0:1, cut : cut + TILE] = jnp.zeros((1, TILE), F32)
            bias[g, 0:1, cut + TILE : cut + 2 * TILE] = jnp.full(
                (1, TILE), jnp.where(filled > 1, 0.0, NEG), F32
            )

    fresh_rows = SIDE * 2 * TILE

    def attend_items(t, part, items):
        for g, (_, reader, _, _) in enumerate(items):
            for source in range(SIDE):
                base = 3 * (zi * SIDE + source)
                flags = [wanted[reader, base + j] for j in range(3)]
                cut = slice(fresh_rows + source * TILE, fresh_rows + (source + 1) * TILE)

                def pick(kind):
                    tile0, tile1, tile2 = [
                        kv[source, kind, (2 + j) * TILE : (3 + j) * TILE] for j in range(3)
                    ]
                    return jnp.where(flags[1] > 0, tile1, jnp.where(flags[2] > 0, tile2, tile0))

                keys[part, g, cut] = pick(2 * part)
                values[part, g, cut, 0:HD] = pick(2 * part + 1)
                used = flags[0] + flags[1] + flags[2]
                bias[g, 0:1, cut] = jnp.full((1, TILE), jnp.where(used > 0, 0.0, NEG), F32)
        scores = [
            lax.dot_general(
                qall[zr, k, pl.ds(starts[t], half)],
                keys[part, g],
                (((1,), (1,)), ((), ())),
                preferred_element_type=F32,
            )
            for g, (zr, _, k, _) in enumerate(items)
        ]
        lane = lax.broadcasted_iota(jnp.int32, (half, HD), 1)
        logs = jnp.zeros((half, HD), F32)
        for g, (_, _, k, place) in enumerate(items):
            score = scores[g] * LOG2_SCALE + bias[g, 0:1, :]
            top = jnp.max(score, axis=1, keepdims=True)
            weight = jnp.exp2(score - top).astype(BF16)
            both = jnp.dot(weight, values[part, g], preferred_element_type=F32)
            total = both[:, HD:]
            o_own[t, place, k] = (both[:, :HD] / total).astype(BF16)
            logs = jnp.where(lane == g, top + jnp.log2(total), logs)
        stats[t, part, 0:half] = logs

    def attend(t, zr, place):
        attend_items(t, 0, [(zr, zr * SIDE + k, k, place) for k in range(last)])
        l_own[t, 0, place] = stats[t, 0].T[0:8, :]

    def attend_last(t):
        places = (zi, z1, z2, z3)
        attend_items(t, 1, [(zr, zr * SIDE + yi, last, i) for i, zr in enumerate(places)])
        logs = stats[t, 1].T[0:8, :]
        for place in range(SIDE):
            l_own[t, 1, place, last : last + 1] = logs[place : place + 1]

    def shares(logs):
        top = functools.reduce(jnp.maximum, logs)
        parts = [jnp.exp2(x - top) for x in logs]
        total = functools.reduce(jnp.add, parts)
        parts = [x / total for x in parts]
        pad = jnp.zeros((HD - 8 * len(logs), LANES), F32)
        return top + jnp.log2(total), jnp.concatenate(parts + [pad], axis=0).T

    def mix(pieces, factors, k):
        mixed = jnp.zeros((half, HD), F32)
        for i, piece in enumerate(pieces):
            mixed += piece.astype(F32) * factors[0:half, 8 * i + k : 8 * i + k + 1]
        return mixed.astype(BF16)

    spans = ((0, last), (last, HEADS))
    near_copies = {}
    far_copies = {}
    row_copies = [[], []]

    def return_near(t, part, place, slot):
        first, stop = spans[part]
        span = pl.ds(first, stop - first)
        copies = near_copies.setdefault((t, part), [])
        copies.append(send(o_own.at[t, place, span], o_near.at[t, slot, span], to_z1))
        copies.append(send(l_own.at[t, part, place], l_near.at[t, part, slot], to_z1))

    def merge(t, part):
        first, stop = spans[part]
        for copy in near_copies[t, part]:
            copy.wait_recv()
        l_merge[t, part], factors = shares([l_own[t, part, 2], l_near[t, part, 1]])
        for k in range(first, stop):
            o_merge[t, k] = mix([o_own[t, 2, k], o_near[t, 1, k]], factors, k)
        span = pl.ds(first, stop - first)
        far_copies[t, part] = [
            send(o_merge.at[t, span], o_far.at[t, span], to_z2),
            send(l_merge.at[t, part], l_far.at[t, part], to_z2),
        ]

    def combine(t, part):
        first, stop = spans[part]
        for copy in far_copies[t, part]:
            copy.wait_recv()
        _, factors = shares([l_own[t, part, 0], l_near[t, part, 0], l_far[t, part]])
        for k in range(first, stop):
            comb[t, k] = mix([o_own[t, 0, k], o_near[t, 0, k], o_far[t, k]], factors, k)
        if part == 0:
            for other, device in row:
                row_copies[t].append(send(comb.at[t, other], att5.at[t, yi], device))
            att5[t, yi] = comb[t, yi]
        else:
            att5[t, last] = comb[t, last]

    part_rows, part_columns = pbuf.shape[3], pbuf.shape[4]
    order = (0, BLOCKS // 2, 1, BLOCKS // 2 + 1)
    plans = {}
    for t in range(HALVES):
        for block in order:
            forward = block < BLOCKS // 2
            ahead, behind = (right, left) if forward else (left, right)
            to_ahead, to_behind = (to_right, to_left) if forward else (to_left, to_right)
            side = 0 if forward else 1
            plans[t, block] = (
                ahead,
                remote(pbuf.at[t, block, opposite], rbuf.at[t, block], to_ahead),
                remote(pbuf.at[t, block, behind], fbuf.at[1 - side, t, block], to_behind),
                remote(pbuf.at[t, block, ahead], fbuf.at[side, t, block], to_ahead),
            )
    hi_plans = {block: remote(zsend.at[block], zrecv.at[block], to_hi) for block in order}

    def project(t):
        for copy in row_copies[t]:
            copy.wait_recv()
        att = jnp.concatenate([att5[t, h] for h in range(HEADS)], axis=1)
        for block in order:
            product = jnp.dot(
                att,
                w[:, block * part_columns : (block + 1) * part_columns],
                preferred_element_type=F32,
            ).astype(BF16)
            for x in range(SIDE):
                pbuf[t, block, x] = product[x * part_rows : (x + 1) * part_rows]
            plans[t, block][1].start()
        for block in order:
            plans[t, block][2].start()

    def relay(t):
        for block in order:
            ahead, far, _, onward = plans[t, block]
            far.wait_recv()
            pbuf[t, block, ahead] = (
                pbuf[t, block, ahead].astype(F32) + rbuf[t, block].astype(F32)
            ).astype(BF16)
            onward.start()

    def reduced(t, block):
        _, _, near, onward = plans[t, block]
        near.wait_recv()
        onward.wait_recv()
        return (
            pbuf[t, block, xi].astype(F32)
            + fbuf[0, t, block].astype(F32)
            + fbuf[1, t, block].astype(F32)
        )

    gather_fresh(0)
    attend(0, zi, 0)
    q_near[0].wait_recv()
    attend(0, z1, 1)
    return_near(0, 0, 1, 0)
    q_relay[0].wait_recv()
    attend(0, z3, 3)
    return_near(0, 0, 3, 1)
    q_far[1].wait_recv()
    q_relay[1] = give_q(1, z2, to_z1)
    attend(0, z2, 2)
    attend(1, zi, 0)
    merge(0, 0)
    q_near[1].wait_recv()
    attend(1, z1, 1)
    return_near(1, 0, 1, 0)
    gather_fresh(1)
    attend_last(0)
    return_near(0, 1, 1, 0)
    return_near(0, 1, 3, 1)
    q_relay[1].wait_recv()
    attend(1, z3, 3)
    return_near(1, 0, 3, 1)
    merge(0, 1)
    attend_last(1)
    return_near(1, 1, 1, 0)
    return_near(1, 1, 3, 1)
    combine(0, 0)
    attend(1, z2, 2)
    combine(0, 1)
    merge(1, 0)
    merge(1, 1)
    w_load.wait()
    project(0)
    relay(0)
    combine(1, 0)
    combine(1, 1)
    project(1)
    for block in order:
        zsend[block] = reduced(0, block).astype(BF16)
        hi_plans[block].start()
    relay(1)
    for block in order:
        total = reduced(1, block)
        hi_plans[block].wait_recv()
        out_ref[:, block * part_columns : (block + 1) * part_columns] = (
            total + zrecv[block].astype(F32)
        ).astype(BF16)
    for copy in started:
        copy.wait_send()


def on_device(
    queries,
    fresh_key,
    fresh_value,
    stale_key,
    stale_value,
    slot_tiles,
    refresh,
    stale_reads,
    out_weight,
):
    tokens, width = queries.shape
    depth, columns = out_weight.shape
    half = tokens // HALVES
    rows = half // SIDE
    cols = columns // BLOCKS
    keys = SIDE * 3 * TILE
    tiles = jnp.arange(refresh.shape[0], dtype=jnp.int32)
    held = (slot_tiles[:, None] == tiles[None, :]).astype(jnp.int32)
    wanted = jnp.sum(stale_reads[:, None, :] * held[None, :, :], axis=2)
    dma = pltpu.SemaphoreType.DMA
    vmem = pltpu.VMEM
    smem_spec = pl.BlockSpec(memory_space=pltpu.SMEM)
    any_spec = pl.BlockSpec(memory_space=pl.ANY)
    copies = 3 + 6 + 6 + HALVES * (8 + 4 + 3 + 3 * BLOCKS) + BLOCKS
    return pl.pallas_call(
        kernel,
        out_shape=jax.ShapeDtypeStruct((rows, columns), BF16),
        in_specs=[smem_spec] * 2 + [any_spec] * 6,
        out_specs=pl.BlockSpec(memory_space=pltpu.VMEM),
        scratch_shapes=[
            vmem((HEADS, tokens, HD), BF16),
            vmem((2, 3, TILE, width), BF16),
            vmem((HEADS, 2, SLOTS * TILE, HD), BF16),
            vmem((SIDE, HEADS, tokens, HD), BF16),
            vmem((SIDE, 4, SLOTS * TILE, HD), BF16),
            vmem((2, GROUP, keys, HD), BF16),
            vmem((2, GROUP, keys, 2 * HD), BF16),
            vmem((GROUP, 8, keys), F32),
            vmem((HALVES, 2, LANES, HD), F32),
            vmem((HALVES, SIDE, HEADS, half, HD), BF16),
            vmem((HALVES, 2, SIDE, 8, LANES), F32),
            vmem((HALVES, 2, HEADS, half, HD), BF16),
            vmem((HALVES, 2, 2, 8, LANES), F32),
            vmem((HALVES, HEADS, half, HD), BF16),
            vmem((HALVES, 2, 8, LANES), F32),
            vmem((HALVES, HEADS, half, HD), BF16),
            vmem((HALVES, 2, 8, LANES), F32),
            vmem((HALVES, HEADS, half, HD), BF16),
            vmem((HALVES, HEADS, half, HD), BF16),
            vmem((depth, columns), BF16),
            vmem((HALVES, BLOCKS, SIDE, rows, cols), BF16),
            vmem((HALVES, BLOCKS, rows, cols), BF16),
            vmem((2, HALVES, BLOCKS, rows, cols), BF16),
            vmem((BLOCKS, rows, cols), BF16),
            vmem((BLOCKS, rows, cols), BF16),
            dma((HEADS * 3 + 3,)),
            dma((copies,)),
            dma((copies,)),
        ],
        compiler_params=pltpu.CompilerParams(
            collective_id=0, has_side_effects=True, vmem_limit_bytes=56 * 2**20
        ),
        name="attend_and_project",
    )(
        refresh,
        wanted,
        queries,
        fresh_key.reshape(3, TILE, width),
        fresh_value.reshape(3, TILE, width),
        stale_key,
        stale_value,
        out_weight,
    )


def solution(mesh):
    return jax.shard_map(
        on_device,
        mesh=mesh,
        in_specs=(
            P(("cfg", "seq"), "head"),
            P(("cfg", "seq"), "head"),
            P(("cfg", "seq"), "head"),
            P(("cfg", "seq"), "head"),
            P(("cfg", "seq"), "head"),
            P("cfg"),
            P("cfg"),
            P("cfg", None),
            P("head", None),
        ),
        out_specs=P(("cfg", "seq", "head"), None),
        check_vma=False,
    )
```

```python
import functools
import math

import jax
import jax.numpy as jnp
from jax import lax
from jax.experimental import pallas as pl
from jax.experimental.pallas import tpu as pltpu
from jax.sharding import PartitionSpec as P

HD = 128
TILE = 128
SIDE = 4
HEADS = 5
SLOTS = 5
HALVES = 2
BLOCKS = 4
GROUP = 4
LANES = 256
MESH = pl.DeviceIdType.MESH
NEG = -1e30
LOG2_SCALE = HD ** (-0.5) * math.log2(math.e)
BF16 = jnp.bfloat16
F32 = jnp.float32


def kernel(
    refresh,
    wanted,
    q_hbm,
    fk_hbm,
    fv_hbm,
    sk_hbm,
    sv_hbm,
    w_hbm,
    out_ref,
    qpack,
    fresh,
    pack,
    qall,
    kv,
    keys,
    values,
    bias,
    stats,
    o_own,
    l_own,
    o_out,
    l_out,
    o_mid,
    l_mid,
    o_mid_send,
    l_mid_send,
    o_back,
    l_back,
    o_back_send,
    l_back_send,
    comb,
    att5,
    w,
    pbuf,
    rbuf,
    fbuf,
    zsend,
    zrecv,
    local_sem,
    send_sem,
    recv_sem,
):
    me = lax.axis_index("seq")
    head = lax.axis_index("head")
    zi, yi = me // SIDE, lax.rem(me, SIDE)
    zh, xi = head // SIDE, lax.rem(head, SIDE)
    right = lax.rem(xi + 1, SIDE)
    left = lax.rem(xi + SIDE - 1, SIDE)
    opposite = lax.rem(xi + 2, SIDE)
    to_right = {"head": zh * SIDE + right}
    to_left = {"head": zh * SIDE + left}
    to_hi = {"head": (1 - zh) * SIDE + xi}
    z1 = zi + 1 - 2 * lax.rem(zi, 2)
    z2 = lax.rem(zi + 2, SIDE)
    z3 = SIDE - 1 - zi
    inner = jnp.logical_or(zi == 1, zi == 2)
    outer = jnp.logical_not(inner)
    zj = jnp.where(inner, z3, z2)
    zp = jnp.where(inner, z2, z3)
    to_z1 = {"seq": z1 * SIDE + yi}
    to_z3 = {"seq": z3 * SIDE + yi}
    row = []
    for step in (2, 1, 3):
        other = lax.rem(yi + step, SIDE)
        row.append((other, {"seq": zi * SIDE + other}))
    last = HEADS - 1
    tokens = qpack.shape[1]
    half = tokens // HALVES
    started = {"all": [], "inner": [], "outer": []}
    count = [0]

    def remote(src, dst, device, role="all"):
        index = count[0]
        count[0] += 1
        copy = pltpu.make_async_remote_copy(
            src_ref=src,
            dst_ref=dst,
            send_sem=send_sem.at[index],
            recv_sem=recv_sem.at[index],
            device_id=device,
            device_id_type=MESH,
        )
        started[role].append(copy)
        return copy

    def send(src, dst, device, role="all"):
        copy = remote(src, dst, device, role)
        copy.start()
        return copy

    local_count = [0]

    def load(src, dst):
        copy = pltpu.make_async_copy(src, dst, local_sem.at[local_count[0]])
        local_count[0] += 1
        copy.start()
        return copy

    def lanes(h):
        return pl.ds(h * HD, HD)

    q_loads = [load(q_hbm.at[:, lanes(h)], qpack.at[h]) for h in range(HEADS)]
    fresh_loads = [load(x, fresh.at[i]) for i, x in enumerate((fk_hbm, fv_hbm))]
    stale_loads = []
    for h in range(HEADS):
        for kind, x in enumerate((sk_hbm, sv_hbm)):
            stale_loads.append(
                load(x.at[:, lanes(h)], pack.at[h, kind, pl.ds(2 * TILE, 3 * TILE)])
            )

    barrier = pltpu.get_barrier_semaphore()
    peers = [device for _, device in row] + [to_z1, to_z3, to_right, to_left, to_hi]
    for device in peers:
        pl.semaphore_signal(barrier, inc=1, device_id=device, device_id_type=MESH)
    pl.semaphore_wait(barrier, len(peers))

    for copy in q_loads:
        copy.wait()
    row_q = [send(qpack.at[other], qall.at[zi, yi], device) for other, device in row]
    qall[zi, yi] = qpack[yi]
    qall[zi, last] = qpack[last]

    r0 = refresh[3 * me]
    r1 = refresh[3 * me + 1]
    r2 = refresh[3 * me + 2]
    for copy in fresh_loads:
        copy.wait()
    for h in range(HEADS):
        for kind in range(2):
            tile0, tile1, tile2 = [fresh[kind, i, :, h * HD : (h + 1) * HD] for i in range(3)]
            pack[h, kind, 0:TILE] = jnp.where(r0 > 0, tile0, jnp.where(r1 > 0, tile1, tile2))
            pack[h, kind, TILE : 2 * TILE] = jnp.where(r2 > 0, tile2, tile1)
    for copy in stale_loads:
        copy.wait()
    row_kv = [
        [send(pack.at[other], kv.at[yi, pl.ds(0, 2)], device) for other, device in row],
        [send(pack.at[last], kv.at[yi, pl.ds(2, 2)], device) for _, device in row],
    ]
    w_load = load(w_hbm, w)
    kv[yi, 0:2] = pack[yi]
    kv[yi, 2:4] = pack[last]
    values[:, :, :, HD:] = jnp.ones((2, GROUP, values.shape[2], HD), BF16)
    stats[...] = jnp.zeros(stats.shape, F32)

    for copy in row_q:
        copy.wait_recv()
    starts = [pl.multiple_of((1 - zh) * half, half), pl.multiple_of(zh * half, half)]

    def give_q(t, zr, device, role):
        part = qall.at[zr, :, pl.ds(starts[t], half)]
        return remote(part, part, device, role)

    q_own = [give_q(t, zi, to_z1, "all") for t in range(HALVES)]
    q_mid = [give_q(t, zi, to_z3, "inner") for t in range(HALVES)]
    q_across = [give_q(t, z1, to_z3, "inner") for t in range(HALVES)]
    q_from_j = [give_q(t, zj, to_z1, "inner") for t in range(HALVES)]
    q_from_p = [give_q(t, zp, to_z1, "inner") for t in range(HALVES)]

    q_own[0].start()

    @pl.when(inner)
    def _():
        q_mid[0].start()

    q_own[0].wait_recv()
    q_own[1].start()

    @pl.when(inner)
    def _():
        q_across[0].start()
        q_mid[0].wait_recv()
        q_from_j[0].start()
        q_mid[1].start()
        q_across[0].wait_recv()
        q_from_p[0].start()

    def gather_fresh(part):
        for copy in row_kv[part]:
            copy.wait_recv()
        for source in range(SIDE):
            cut = slice(source * 2 * TILE, (source + 1) * 2 * TILE)
            fresh_keys = kv[source, 2 * part, 0 : 2 * TILE]
            fresh_values = kv[source, 2 * part + 1, 0 : 2 * TILE]
            for g in range(GROUP):
                keys[part, g, cut] = fresh_keys
                values[part, g, cut, 0:HD] = fresh_values

    for source in range(SIDE):
        base = 3 * (zi * SIDE + source)
        filled = refresh[base] + refresh[base + 1] + refresh[base + 2]
        cut = source * 2 * TILE
        for g in range(GROUP):
            bias[g, 0:1, cut : cut + TILE] = jnp.zeros((1, TILE), F32)
            bias[g, 0:1, cut + TILE : cut + 2 * TILE] = jnp.full(
                (1, TILE), jnp.where(filled > 1, 0.0, NEG), F32
            )

    fresh_rows = SIDE * 2 * TILE

    def attend_items(t, part, items):
        for g, (_, reader, _, _) in enumerate(items):
            for source in range(SIDE):
                base = 3 * (zi * SIDE + source)
                flags = [wanted[reader, base + j] for j in range(3)]
                cut = slice(fresh_rows + source * TILE, fresh_rows + (source + 1) * TILE)

                def pick(kind):
                    tile0, tile1, tile2 = [
                        kv[source, kind, (2 + j) * TILE : (3 + j) * TILE] for j in range(3)
                    ]
                    return jnp.where(flags[1] > 0, tile1, jnp.where(flags[2] > 0, tile2, tile0))

                keys[part, g, cut] = pick(2 * part)
                values[part, g, cut, 0:HD] = pick(2 * part + 1)
                used = flags[0] + flags[1] + flags[2]
                bias[g, 0:1, cut] = jnp.full((1, TILE), jnp.where(used > 0, 0.0, NEG), F32)
        scores = [
            lax.dot_general(
                qall[zr, k, pl.ds(starts[t], half)],
                keys[part, g],
                (((1,), (1,)), ((), ())),
                preferred_element_type=F32,
            )
            for g, (zr, _, k, _) in enumerate(items)
        ]
        lane = lax.broadcasted_iota(jnp.int32, (half, HD), 1)
        logs = jnp.zeros((half, HD), F32)
        for g, (_, _, k, place) in enumerate(items):
            score = scores[g] * LOG2_SCALE + bias[g, 0:1, :]
            top = jnp.max(score, axis=1, keepdims=True)
            weight = jnp.exp2(score - top).astype(BF16)
            both = jnp.dot(weight, values[part, g], preferred_element_type=F32)
            total = both[:, HD:]
            o_own[t, place, k] = (both[:, :HD] / total).astype(BF16)
            logs = jnp.where(lane == g, top + jnp.log2(total), logs)
        stats[t, part, 0:half] = logs

    def attend(t, zr, place):
        attend_items(t, 0, [(zr, zr * SIDE + k, k, place) for k in range(last)])
        l_own[t, 0, place] = stats[t, 0].T[0:8, :]

    def attend_last(t):
        places = (zi, z1, zj, zp)
        attend_items(t, 1, [(zr, zr * SIDE + yi, last, i) for i, zr in enumerate(places)])
        logs = stats[t, 1].T[0:8, :]
        for place in range(SIDE):
            l_own[t, 1, place, last : last + 1] = logs[place : place + 1]

    def shares(logs):
        top = functools.reduce(jnp.maximum, logs)
        parts = [jnp.exp2(x - top) for x in logs]
        total = functools.reduce(jnp.add, parts)
        parts = [x / total for x in parts]
        pad = jnp.zeros((HD - 8 * len(logs), LANES), F32)
        return top + jnp.log2(total), jnp.concatenate(parts + [pad], axis=0).T

    def mix(pieces, factors, k):
        mixed = jnp.zeros((half, HD), F32)
        for i, piece in enumerate(pieces):
            mixed += piece.astype(F32) * factors[0:half, 8 * i + k : 8 * i + k + 1]
        return mixed.astype(BF16)

    spans = ((0, last), (last, HEADS))
    row_copies = [[], []]

    def pair(o_src, l_src, o_dst, l_dst, device, role):
        return [remote(o_src, o_dst, device, role), remote(l_src, l_dst, device, role)]

    out_copies, mid_copies, back_copies = {}, {}, {}
    for t in range(HALVES):
        for part, (first, stop) in enumerate(spans):
            span = pl.ds(first, stop - first)
            for place in (1, 2, 3):
                out_copies[t, part, place] = pair(
                    o_own.at[t, place, span],
                    l_own.at[t, part, place],
                    o_out.at[t, place - 1, span],
                    l_out.at[t, part, place - 1],
                    to_z1,
                    "outer",
                )
            for i in range(2):
                mid_copies[t, part, i] = pair(
                    o_mid_send.at[t, i, span],
                    l_mid_send.at[t, part, i],
                    o_mid.at[t, i, span],
                    l_mid.at[t, part, i],
                    to_z3,
                    "inner",
                )
            back_copies[t, part] = pair(
                o_back_send.at[t, span],
                l_back_send.at[t, part],
                o_back.at[t, span],
                l_back.at[t, part],
                to_z1,
                "inner",
            )

    def start(copies):
        for copy in copies:
            copy.start()

    def arrive(copies):
        for copy in copies:
            copy.wait_recv()

    def give_out(t, part, *places):
        @pl.when(outer)
        def _():
            for place in places:
                start(out_copies[t, part, place])

    def merge(t, part):
        @pl.when(inner)
        def _():
            for i, place in ((1, 3), (0, 2)):
                arrive(out_copies[t, part, place])
                log, factors = shares([l_own[t, part, place], l_out[t, part, place - 1]])
                l_mid_send[t, part, i] = log
                for k in range(*spans[part]):
                    o_mid_send[t, i, k] = mix(
                        [o_own[t, place, k], o_out[t, place - 1, k]], factors, k
                    )
                start(mid_copies[t, part, i])

    def give_back(t, part):
        @pl.when(inner)
        def _():
            arrive(mid_copies[t, part, 1])
            log, factors = shares([l_own[t, part, 1], l_mid[t, part, 1]])
            l_back_send[t, part] = log
            for k in range(*spans[part]):
                o_back_send[t, k] = mix([o_own[t, 1, k], o_mid[t, 1, k]], factors, k)
            start(back_copies[t, part])

    def combine(t, part):
        @pl.when(inner)
        def _():
            arrive(out_copies[t, part, 1])
            arrive(mid_copies[t, part, 0])
            _, factors = shares([l_own[t, part, 0], l_out[t, part, 0], l_mid[t, part, 0]])
            for k in range(*spans[part]):
                comb[t, k] = mix([o_own[t, 0, k], o_out[t, 0, k], o_mid[t, 0, k]], factors, k)

        @pl.when(outer)
        def _():
            arrive(back_copies[t, part])
            _, factors = shares([l_own[t, part, 0], l_back[t, part]])
            for k in range(*spans[part]):
                comb[t, k] = mix([o_own[t, 0, k], o_back[t, k]], factors, k)

        if part == 0:
            for other, device in row:
                row_copies[t].append(send(comb.at[t, other], att5.at[t, yi], device))
            att5[t, yi] = comb[t, yi]
        else:
            att5[t, last] = comb[t, last]

    part_rows, part_columns = pbuf.shape[3], pbuf.shape[4]
    order = (0, BLOCKS // 2, 1, BLOCKS // 2 + 1)
    plans = {}
    for t in range(HALVES):
        for block in order:
            forward = block < BLOCKS // 2
            ahead, behind = (right, left) if forward else (left, right)
            to_ahead, to_behind = (to_right, to_left) if forward else (to_left, to_right)
            side = 0 if forward else 1
            plans[t, block] = (
                ahead,
                remote(pbuf.at[t, block, opposite], rbuf.at[t, block], to_ahead),
                remote(pbuf.at[t, block, behind], fbuf.at[1 - side, t, block], to_behind),
                remote(pbuf.at[t, block, ahead], fbuf.at[side, t, block], to_ahead),
            )
    hi_plans = {block: remote(zsend.at[block], zrecv.at[block], to_hi) for block in order}

    def project(t):
        for copy in row_copies[t]:
            copy.wait_recv()
        att = jnp.concatenate([att5[t, h] for h in range(HEADS)], axis=1)
        for block in order:
            product = jnp.dot(
                att,
                w[:, block * part_columns : (block + 1) * part_columns],
                preferred_element_type=F32,
            ).astype(BF16)
            for x in range(SIDE):
                pbuf[t, block, x] = product[x * part_rows : (x + 1) * part_rows]
            plans[t, block][1].start()
        for block in order:
            plans[t, block][2].start()

    def relay(t):
        for block in order:
            ahead, far, _, onward = plans[t, block]
            far.wait_recv()
            pbuf[t, block, ahead] = (
                pbuf[t, block, ahead].astype(F32) + rbuf[t, block].astype(F32)
            ).astype(BF16)
            onward.start()

    def reduced(t, block):
        _, _, near, onward = plans[t, block]
        near.wait_recv()
        onward.wait_recv()
        return (
            pbuf[t, block, xi].astype(F32)
            + fbuf[0, t, block].astype(F32)
            + fbuf[1, t, block].astype(F32)
        )

    gather_fresh(0)
    attend(0, zi, 0)

    @pl.when(outer)
    def _():
        q_from_p[0].wait_recv()

    attend(0, zp, 3)
    give_out(0, 0, 3)
    q_own[1].wait_recv()

    @pl.when(inner)
    def _():
        q_across[1].start()
        q_mid[1].wait_recv()
        q_from_j[1].start()

    @pl.when(outer)
    def _():
        q_from_j[0].wait_recv()

    attend(0, zj, 2)
    give_out(0, 0, 2)

    @pl.when(inner)
    def _():
        q_across[1].wait_recv()
        q_from_p[1].start()

    attend(0, z1, 1)
    give_out(0, 0, 1)
    attend(1, zi, 0)

    @pl.when(outer)
    def _():
        q_from_j[1].wait_recv()

    attend(1, zj, 2)
    give_out(1, 0, 2)
    merge(0, 0)
    gather_fresh(1)
    attend_last(0)
    give_out(0, 1, 3, 2, 1)

    @pl.when(outer)
    def _():
        q_from_p[1].wait_recv()

    attend(1, zp, 3)
    give_out(1, 0, 3)
    merge(0, 1)
    attend(1, z1, 1)
    give_out(1, 0, 1)
    give_back(0, 0)
    attend_last(1)
    give_out(1, 1, 3, 2, 1)
    give_back(0, 1)
    combine(0, 0)
    combine(0, 1)
    merge(1, 0)
    merge(1, 1)
    w_load.wait()
    project(0)
    give_back(1, 0)
    give_back(1, 1)
    relay(0)
    combine(1, 0)
    combine(1, 1)
    project(1)
    for block in order:
        zsend[block] = reduced(0, block).astype(BF16)
        hi_plans[block].start()
    relay(1)
    for block in order:
        total = reduced(1, block)
        hi_plans[block].wait_recv()
        out_ref[:, block * part_columns : (block + 1) * part_columns] = (
            total + zrecv[block].astype(F32)
        ).astype(BF16)
    for copy in started["all"]:
        copy.wait_send()

    @pl.when(inner)
    def _():
        for copy in started["inner"]:
            copy.wait_send()

    @pl.when(outer)
    def _():
        for copy in started["outer"]:
            copy.wait_send()


def on_device(
    queries,
    fresh_key,
    fresh_value,
    stale_key,
    stale_value,
    slot_tiles,
    refresh,
    stale_reads,
    out_weight,
):
    tokens, width = queries.shape
    depth, columns = out_weight.shape
    half = tokens // HALVES
    rows = half // SIDE
    cols = columns // BLOCKS
    keys = SIDE * 3 * TILE
    tiles = jnp.arange(refresh.shape[0], dtype=jnp.int32)
    held = (slot_tiles[:, None] == tiles[None, :]).astype(jnp.int32)
    wanted = jnp.sum(stale_reads[:, None, :] * held[None, :, :], axis=2)
    dma = pltpu.SemaphoreType.DMA
    vmem = pltpu.VMEM
    smem_spec = pl.BlockSpec(memory_space=pltpu.SMEM)
    any_spec = pl.BlockSpec(memory_space=pl.ANY)
    copies = 3 + 6 + 10 + HALVES * (12 + 8 + 4 + 3 + 3 * BLOCKS) + BLOCKS
    return pl.pallas_call(
        kernel,
        out_shape=jax.ShapeDtypeStruct((rows, columns), BF16),
        in_specs=[smem_spec] * 2 + [any_spec] * 6,
        out_specs=pl.BlockSpec(memory_space=pltpu.VMEM),
        scratch_shapes=[
            vmem((HEADS, tokens, HD), BF16),
            vmem((2, 3, TILE, width), BF16),
            vmem((HEADS, 2, SLOTS * TILE, HD), BF16),
            vmem((SIDE, HEADS, tokens, HD), BF16),
            vmem((SIDE, 4, SLOTS * TILE, HD), BF16),
            vmem((2, GROUP, keys, HD), BF16),
            vmem((2, GROUP, keys, 2 * HD), BF16),
            vmem((GROUP, 8, keys), F32),
            vmem((HALVES, 2, LANES, HD), F32),
            vmem((HALVES, SIDE, HEADS, half, HD), BF16),
            vmem((HALVES, 2, SIDE, 8, LANES), F32),
            vmem((HALVES, 3, HEADS, half, HD), BF16),
            vmem((HALVES, 2, 3, 8, LANES), F32),
            vmem((HALVES, 2, HEADS, half, HD), BF16),
            vmem((HALVES, 2, 2, 8, LANES), F32),
            vmem((HALVES, 2, HEADS, half, HD), BF16),
            vmem((HALVES, 2, 2, 8, LANES), F32),
            vmem((HALVES, HEADS, half, HD), BF16),
            vmem((HALVES, 2, 8, LANES), F32),
            vmem((HALVES, HEADS, half, HD), BF16),
            vmem((HALVES, 2, 8, LANES), F32),
            vmem((HALVES, HEADS, half, HD), BF16),
            vmem((HALVES, HEADS, half, HD), BF16),
            vmem((depth, columns), BF16),
            vmem((HALVES, BLOCKS, SIDE, rows, cols), BF16),
            vmem((HALVES, BLOCKS, rows, cols), BF16),
            vmem((2, HALVES, BLOCKS, rows, cols), BF16),
            vmem((BLOCKS, rows, cols), BF16),
            vmem((BLOCKS, rows, cols), BF16),
            dma((HEADS * 3 + 3,)),
            dma((copies,)),
            dma((copies,)),
        ],
        compiler_params=pltpu.CompilerParams(
            collective_id=0, has_side_effects=True, vmem_limit_bytes=56 * 2**20
        ),
        name="attend_and_project",
    )(
        refresh,
        wanted,
        queries,
        fresh_key.reshape(3, TILE, width),
        fresh_value.reshape(3, TILE, width),
        stale_key,
        stale_value,
        out_weight,
    )


def solution(mesh):
    return jax.shard_map(
        on_device,
        mesh=mesh,
        in_specs=(
            P(("cfg", "seq"), "head"),
            P(("cfg", "seq"), "head"),
            P(("cfg", "seq"), "head"),
            P(("cfg", "seq"), "head"),
            P(("cfg", "seq"), "head"),
            P("cfg"),
            P("cfg"),
            P("cfg", None),
            P("head", None),
        ),
        out_specs=P(("cfg", "seq", "head"), None),
        check_vma=False,
    )
```
